32 devices in a mesh: dp: 4 (over z), node: 4 (over y, x), local: 2 (over core).
Axes of the slice: x: 2, y: 2, z: 4, core: 2. Of those that a mesh axis runs over, the one named last changes fastest.
Arguments:
- tokens: bfloat16 [128, 3584], P(('dp', 'node', 'local')), may hold values from -6 to 6
- routes: int32 [128, 2], P(('dp', 'node', 'local')), may hold values from 0 to 3, all different within a row; in each aligned block of 32 rows (0 to 31, 32 to 63, ...) at most 32 rows name the same one
- gate_fix: int32 [128, 2], P(('dp', 'node', 'local')), may hold values from 1 to 65535
- keep: int32 [128, 2], P(('dp', 'node', 'local')), may hold values 0 or 1
- seq_lengths: int32 [4, 2], P('dp'), may hold values from 1024 to 4096, as said below
- cotangent: bfloat16 [128, 3584], P(('dp', 'node', 'local')), may hold values from -6 to 6
- w_gate: bfloat16 [4, 1024, 3584], P('dp', ('node', 'local')), may hold values from -0.09375 to 0.09375
- w_up: bfloat16 [4, 1024, 3584], P('dp', ('node', 'local')), may hold values from -0.09375 to 0.09375
- w_down: bfloat16 [4, 1024, 3584], P('dp', ('node', 'local')), may hold values from -0.1875 to 0.1875
Outputs:
- layer_out: bfloat16 [128, 3584], P(('dp', 'node', 'local'))
- token_grad: bfloat16 [128, 3584], P(('dp', 'node', 'local'))
- grad_gate: bfloat16 [4, 1024, 3584], P('dp', ('node', 'local'))
- grad_down: bfloat16 [4, 1024, 3584], P('dp', ('node', 'local'))
The draws below stay inside these ranges and needn't reach their ends.
Inputs may be any that keep to these rules, and one draw needn't show every extreme that they name: In each aligned block of 32 rows (the tokens of one group) no expert is named by more than 32 routes, a bound that some block reaches. `seq_lengths`: the chosen sequence of the first group counts all 4096 positions.
All inputs are finite; a program needn't handle non-finite values. No bound on the sum of `keep` on one device may be relied on, other than what follows from the above.
Results may differ from the reference program's by a relative error of at most 0.013.
Values may be sent and summed in bfloat16 or wider, within the bound.
A program may use at most 64 MiB of HBM per device.

```python
import math
import jax
import jax.numpy as jnp
import numpy as np
from jax import lax

D = 3584
FF = 1024
SEQ = 4096
TOK_DEV = 4
EXPERTS = 4
TOPK = 2
GROUP_TOK = 32
CAP = 32
SPAN = 1024
GROUPS = 4
TOKENS = 128
N_NODE = 4
N_LOCAL = 2


def draw_seq_lengths(key, part):
    key = jax.random.fold_in(key, 7)
    values = jax.random.randint(key, (GROUPS, 2), SEQ // 4, SEQ + 1, dtype=jnp.int32)
    return values.at[0, 0].set(SEQ)


def place_ends(result, key, least, top_value):
    shape = result.shape
    spot = [jax.random.randint(jax.random.fold_in(key, axis), (), 0, shape[axis]) for axis in range(len(shape))]
    result = result.at[tuple(spot)].set(least)
    longest = shape.index(max(shape))
    spot[longest] = (spot[longest] + 1) % shape[longest]
    return result.at[tuple(spot)].set(top_value)


def block_scale(own_key, dims, split, smallest, top_value):
    loudness = 1.0
    for dim, blocks in split:
        draws = jax.random.uniform(jax.random.fold_in(jax.random.fold_in(own_key, 6), dim), (blocks,), jnp.float32, smallest / len(split), top_value / len(split))
        loudness = loudness * jnp.repeat(jnp.exp(draws), dims[dim] // blocks).reshape((-1,) + (1,) * (len(dims) - 1 - dim))
    return loudness


def deal_out(rng, own, number, rows, number_of, top, reach, slope):
    sequence = jax.random.permutation(rng, number_of)
    crowded, common = shares(number_of, rows * top, reach, slope, True), shares(number_of, rows * top, reach, slope, False)
    places = jnp.arange(number_of)

    def named(sizes, rotation):
        used = int((sizes > 0).sum())
        fixed = max(1, used // 4)
        passed = fixed + (places - fixed + rotation * (used - fixed)) % max(1, number_of - fixed)
        return jnp.zeros((number_of,), jnp.int32).at[sequence[jnp.where(places < fixed, places, passed)]].set(jnp.asarray(sizes, jnp.int32))

    sizes = jnp.where(number % 4 == 0, named(crowded, number // 4), named(common, number - number // 4 - 1))
    mixed = jax.random.permutation(jax.random.fold_in(own, 3), number_of)
    donor, receiver = mixed[0:number_of // 2 * 2:2], mixed[1:number_of // 2 * 2:2]
    margin = jnp.minimum(sizes[donor] - 1, reach - sizes[receiver]) // 2
    margin = jnp.where((donor == sequence[0]) | (receiver == sequence[0]) | (sizes[receiver] == 0), 0, jnp.maximum(margin, 0))
    passed = jax.random.randint(jax.random.fold_in(own, 4), (number_of // 2,), 0, 1 << 20) % (margin + 1)
    sizes = sizes.at[donor].add(-passed).at[receiver].add(passed)
    labels = jnp.searchsorted(jnp.cumsum(sizes), jnp.arange(rows * top), side="right").astype(jnp.int32)
    table = labels.reshape(top, rows).T
    table = table[jax.random.permutation(jax.random.fold_in(own, 1), rows)]
    rotation = jax.random.randint(jax.random.fold_in(own, 2), (rows, 1), 0, top)
    return jnp.take_along_axis(table, (jnp.arange(top)[None, :] + rotation) % top, axis=1)


def shares(amount, total, reach, lean, full):
    loads = [(1 << 20) // math.isqrt(rank ** lean) + 1 for rank in range(1, amount + 1)]
    largest = reach if full else min(reach, max(-(-total // amount), total * loads[0] // sum(loads)))
    least = 1 if total - largest >= amount - 1 else 0
    holding, rest = [largest] + [least] * (amount - 1), total - largest - least * (amount - 1)
    while rest > 0:
        movable = [i for i in range(1, amount) if holding[i] < largest] or [i for i in range(1, amount) if holding[i] < reach]
        whole, left = sum([loads[i] for i in movable]), rest
        for i in movable:
            more = min(reach - holding[i], max(1, left * loads[i] // whole), rest)
            holding[i] = holding[i] + more
            rest = rest - more
    return np.array(holding)


def centred(stream_key, extent, width, reach, split=(), kind=jnp.bfloat16):
    entries = width * jax.random.normal(stream_key, extent, jnp.float32)
    if split:
        entries = entries * block_scale(stream_key, extent, split, -0.22, 0.18)
    return jnp.clip(entries, -reach, reach).astype(kind)


def setup_inputs(seed: int = 0) -> dict:
    key_of = jax.random.split(jax.random.key(seed), 10)
    tokens = centred(key_of[0], (TOKENS, D), 1.0, 6.0, ((0, 32),))
    routes_keys = jax.random.split(jax.random.fold_in(key_of[1], 1), TOKENS // GROUP_TOK)
    routes_turns = jax.random.permutation(jax.random.fold_in(key_of[1], 3), TOKENS // GROUP_TOK)
    routes = jax.vmap(lambda own, number: deal_out(jax.random.fold_in(key_of[1], 2), own, number, GROUP_TOK, EXPERTS, TOPK, CAP, 2))(routes_keys, routes_turns).reshape((TOKENS, TOPK))
    gate_fix = place_ends(jax.random.randint(key_of[2], (TOKENS, TOPK), 1, 65536), jax.random.fold_in(key_of[2], 1), 1, 65535).astype(jnp.int32)
    keep = place_ends((jax.random.randint(key_of[3], (TOKENS, TOPK), 0, 4) < 3).astype(jnp.int32), jax.random.fold_in(key_of[3], 1), 0, 1)
    seq_lengths = draw_seq_lengths(jax.random.fold_in(key_of[9], 71), 0)
    cotangent = centred(key_of[5], (TOKENS, D), 1.0, 6.0, ((0, 32),))
    w_gate = centred(key_of[6], (EXPERTS, FF, D), D ** -0.5, 0.09375, ((0, 4), (1, 8)))
    w_up = centred(key_of[7], (EXPERTS, FF, D), D ** -0.5, 0.09375, ((0, 4), (1, 8)))
    w_down = centred(key_of[8], (EXPERTS, FF, D), FF ** -0.5, 0.1875, ((0, 4), (1, 8)))
    return dict(tokens=tokens, routes=routes, gate_fix=gate_fix, keep=keep, seq_lengths=seq_lengths, cotangent=cotangent, w_gate=w_gate, w_up=w_up, w_down=w_down)


gate_unit = 1.0 / 65536.0


def route_tables(route_ids, weight_fix, experts, capacity):
    tok_rows, topk = route_ids.shape
    flat_ids = route_ids.reshape(-1).astype(jnp.int32)
    onehot = (flat_ids[:, None] == jnp.arange(experts, dtype=jnp.int32)[None, :]).astype(jnp.int32)
    before = jnp.cumsum(onehot, axis=0) - onehot
    slot_index = jnp.sum(before * onehot, axis=1)
    target = flat_ids * capacity + slot_index
    places = jnp.arange(experts * capacity, dtype=jnp.int32)
    hit_table = (target[:, None] == places[None, :]).reshape(tok_rows, topk, experts * capacity)
    weight = (weight_fix.astype(jnp.float32) * gate_unit).reshape(tok_rows, topk, 1)
    select = jnp.any(hit_table, axis=1)
    combine = jnp.sum(jnp.where(hit_table, weight, jnp.float32(0.0)), axis=1)
    return select, combine


def token_scale(position, lengths, seq):
    seq_id = position // seq
    inside = position - seq_id * seq
    length = jnp.where(seq_id == 0, lengths[0], lengths[1]).astype(jnp.int32)
    valid = (inside < length).astype(jnp.float32)
    sign = (1 - 2 * seq_id).astype(jnp.float32)
    return sign * valid * jnp.float32(seq) / length.astype(jnp.float32)


def shard_sum(pairs, parts):
    total = None
    for left, right in pairs:
        rows = left.shape[0]
        runs = left.shape[1] // parts
        left_q = left.reshape(rows, parts, runs).transpose(1, 0, 2).astype(jnp.float32)
        right_q = right.reshape(parts, runs, right.shape[1]).astype(jnp.float32)
        term = jnp.einsum("qrf,qfd->qrd", left_q, right_q)
        total = term if total is None else total + term
    rounded = lax.optimization_barrier(total.astype(jnp.bfloat16))
    return jnp.sum(rounded.astype(jnp.float32), axis=0)


def expert_pass(rows_x, rows_g, gate_slice, up_slice, down_slice, parts):
    gate_pre = jnp.dot(rows_x, gate_slice.T, preferred_element_type=jnp.float32)
    up_pre = jnp.dot(rows_x, up_slice.T, preferred_element_type=jnp.float32)
    sig_gate = jax.nn.sigmoid(gate_pre)
    silu_gate = gate_pre * sig_gate
    hidden = (silu_gate * up_pre).astype(jnp.bfloat16)
    expert_out = shard_sum([(hidden, down_slice)], parts).astype(jnp.bfloat16)
    hidden_grad = jnp.dot(rows_g, down_slice.T, preferred_element_type=jnp.float32)
    dsilu = sig_gate * (1.0 + gate_pre * (1.0 - sig_gate))
    gate_delta = (hidden_grad * up_pre * dsilu).astype(jnp.bfloat16)
    up_delta = (hidden_grad * silu_gate).astype(jnp.bfloat16)
    row_grad = shard_sum([(gate_delta, gate_slice), (up_delta, up_slice)], parts).astype(jnp.bfloat16)
    part_gate = jnp.dot(gate_delta.T, rows_x, preferred_element_type=jnp.float32).astype(jnp.bfloat16)
    part_down = jnp.dot(hidden.T, rows_g, preferred_element_type=jnp.float32).astype(jnp.bfloat16)
    return expert_out, row_grad, part_gate, part_down


def reference(tokens, routes, gate_fix, keep, seq_lengths, cotangent, w_gate, w_up, w_down):
    rank_count = N_NODE * N_LOCAL
    group_tok = TOK_DEV * rank_count
    block_x = tokens.reshape(GROUPS, group_tok, D)
    block_c = cotangent.reshape(GROUPS, group_tok, D)
    block_r = routes.reshape(GROUPS, group_tok, TOPK)
    block_w = (keep * gate_fix).reshape(GROUPS, group_tok, TOPK)
    select, combine = jax.vmap(lambda r, w: route_tables(r, w, EXPERTS, CAP))(block_r, block_w)
    member = jnp.arange(group_tok, dtype=jnp.int32)
    position = (member // TOK_DEV) * SPAN + (member % TOK_DEV) * (SPAN // TOK_DEV)
    factor = jax.vmap(lambda lengths: token_scale(position, lengths, SEQ))(seq_lengths)

    def build(items):
        sel, comb, scale_rows, rows, cot = items
        sent = jnp.dot(sel.astype(jnp.bfloat16).T, rows, preferred_element_type=jnp.float32).astype(jnp.bfloat16)
        upstream = jnp.dot((comb * scale_rows[:, None]).T, cot.astype(jnp.float32),
                           precision=lax.Precision.HIGHEST).astype(jnp.bfloat16)
        return sent, upstream

    sent_x, sent_g = lax.map(build, (select, combine, factor, block_x, block_c))
    recv_x = sent_x.reshape(GROUPS, EXPERTS, CAP, D).transpose(1, 0, 2, 3).reshape(EXPERTS, GROUPS * CAP, D)
    recv_g = sent_g.reshape(GROUPS, EXPERTS, CAP, D).transpose(1, 0, 2, 3).reshape(EXPERTS, GROUPS * CAP, D)
    expert_out, row_grad, grad_gate, grad_down = lax.map(
        lambda items: expert_pass(*items, rank_count), (recv_x, recv_g, w_gate, w_up, w_down))
    back_o = expert_out.reshape(EXPERTS, GROUPS, CAP, D).transpose(1, 0, 2, 3).reshape(GROUPS, EXPERTS * CAP, D)
    back_d = row_grad.reshape(EXPERTS, GROUPS, CAP, D).transpose(1, 0, 2, 3).reshape(GROUPS, EXPERTS * CAP, D)

    def finish(items):
        sel, comb, rows_o, rows_d = items
        mixed = jnp.dot(comb, rows_o.astype(jnp.float32), precision=lax.Precision.HIGHEST).astype(jnp.bfloat16)
        grads = jnp.dot(sel.astype(jnp.bfloat16), rows_d, preferred_element_type=jnp.float32).astype(jnp.bfloat16)
        return mixed, grads

    mixed, grads = lax.map(finish, (select, combine, back_o, back_d))
    return (mixed.reshape(TOKENS, D), grads.reshape(TOKENS, D), grad_gate, grad_down)
```

```python
import functools

import jax
import jax.numpy as jnp
from jax import lax
from jax.experimental import pallas as pl
from jax.experimental.pallas import tpu as pltpu
from jax.sharding import PartitionSpec as P

SEQ = 4096
LANES = 128
PIECES = 4
AXES = ("dp", "node", "local")

bf16, f32, i32 = jnp.bfloat16, jnp.float32, jnp.int32


class Flow:
    def __init__(self, buf, first, second, sizes, width, sems):
        self.buf, self.first, self.second = buf, first, second
        self.n1, self.n2 = sizes[first], sizes[second]
        self.i1, self.i2 = lax.axis_index(first), lax.axis_index(second)
        self.core = lax.axis_index("local")
        self.width = width
        self.s1, self.q1, self.s2, self.q2, self.s0, self.q0 = sems[:6]
        self.t1, self.u1, self.t2, self.u2, self.t0, self.u0 = sems[6:]
        self.sent = []

    def push(self, src, dst, send, recv, axis, peer):
        copy = pltpu.make_async_remote_copy(
            src_ref=src, dst_ref=dst, send_sem=send, recv_sem=recv,
            device_id={axis: peer}, device_id_type=pl.DeviceIdType.MESH,
        )
        copy.start()
        self.sent.append(copy)

    def arrive(self, dst, send, recv, axis, peer):
        pltpu.make_async_remote_copy(
            src_ref=dst, dst_ref=dst, send_sem=send, recv_sem=recv,
            device_id={axis: peer}, device_id_type=pl.DeviceIdType.MESH,
        ).wait_recv()

    def drain(self):
        for copy in self.sent:
            copy.wait_send()
        self.sent = []

    def gather_first(self):
        own = self.buf.at[self.core, self.i2, self.i1]
        for k in range(1, self.n1):
            self.push(own, own, self.s1.at[k], self.q1.at[k], self.first, lax.rem(self.i1 + k, self.n1))

    def gather_second(self):
        for k in range(1, self.n1):
            source = lax.rem(self.i1 + self.n1 - k, self.n1)
            self.arrive(self.buf.at[self.core, self.i2, source], self.s1.at[k], self.q1.at[k], self.first, source)
        own = self.buf.at[self.core, self.i2]
        for k in range(1, self.n2):
            self.push(own, own, self.s2.at[k], self.q2.at[k], self.second, lax.rem(self.i2 + k, self.n2))
        self.push(own, own, self.s0.at[0], self.q0.at[0], "local", 1 - self.core)

    def gather_core(self):
        for k in range(1, self.n2):
            source = lax.rem(self.i2 + self.n2 - k, self.n2)
            block = self.buf.at[self.core, source]
            self.arrive(block, self.s2.at[k], self.q2.at[k], self.second, source)
            self.push(block, block, self.s0.at[k], self.q0.at[k], "local", 1 - self.core)

    def gathered(self):
        for k in range(self.n2):
            source = lax.rem(self.i2 + self.n2 - k, self.n2)
            block = self.buf.at[1 - self.core, source]
            self.arrive(block, self.s0.at[k], self.q0.at[k], "local", 1 - self.core)

    def lanes(self, *index):
        return self.buf.at[(*index, Ellipsis, pl.ds(0, self.width))]

    def sum_core(self, r0):
        self.push(self.lanes(1 - self.core), r0, self.t0, self.u0, "local", 1 - self.core)

    def sum_second(self, r0, r1):
        self.arrive(r0, self.t0, self.u0, "local", 1 - self.core)
        for k in list(range(1, self.n2)) + [0]:
            peer = lax.rem(self.i2 + k, self.n2)
            kept = self.lanes(self.core, peer)
            kept[...] = (kept[...].astype(f32) + r0[peer].astype(f32)).astype(bf16)
            if k:
                self.push(kept, r1.at[k - 1], self.t2.at[k], self.u2.at[k], self.second, peer)

    def sum_first(self, r1, r2):
        kept = self.lanes(self.core, self.i2)
        for k in range(1, self.n2):
            source = lax.rem(self.i2 + self.n2 - k, self.n2)
            self.arrive(r1.at[k - 1], self.t2.at[k], self.u2.at[k], self.second, source)
        total = kept[...].astype(f32)
        for k in range(1, self.n2):
            total = total + r1[k - 1].astype(f32)
        kept[...] = total.astype(bf16)
        for k in range(1, self.n1):
            peer = lax.rem(self.i1 + k, self.n1)
            self.push(self.lanes(self.core, self.i2, peer), r2.at[k - 1], self.t1.at[k], self.u1.at[k], self.first, peer)

    def summed(self, r2):
        total = self.lanes(self.core, self.i2, self.i1)[...].astype(f32)
        for k in range(1, self.n1):
            source = lax.rem(self.i1 + self.n1 - k, self.n1)
            self.arrive(r2.at[k - 1], self.t1.at[k], self.u1.at[k], self.first, source)
            total = total + r2[k - 1].astype(f32)
        return total


def kernel(sizes, tok, routes, fix, keep, lens, cot, wg_hbm, wu_hbm, wd_hbm,
           layer_out, token_grad, grad_gate, grad_down,
           buf_a, buf_b, stage, wg, wu, wd, xs, gs, cw, fw, back, hid, gd,
           r0a, r1a, r2a, r0b, r1b, r2b, wsem, *sems):
    nd, nn, nl = (sizes[a] for a in AXES)
    me_d, me_n, me_l = (lax.axis_index(a) for a in AXES)
    rows, width = tok.shape
    topk = routes.shape[1]
    piece = width // PIECES
    ranks = nn * nl
    group = rows * ranks
    chunk = rows * PIECES
    block = ranks * chunk
    span = 2 * SEQ // ranks
    total_rows = nd * group
    a = Flow(buf_a, "dp", "node", sizes, piece, sems[:12])
    b = Flow(buf_b, "node", "dp", sizes, piece, sems[12:])

    loads = [pltpu.make_async_copy(src, dst, wsem.at[k])
             for k, (src, dst) in enumerate(((wg_hbm, wg), (wu_hbm, wu), (wd_hbm, wd)))]
    for load in loads:
        load.start()

    barrier = pltpu.get_barrier_semaphore()
    for axis in AXES:
        for k in range(1, sizes[axis]):
            pl.semaphore_signal(barrier, inc=1, device_id={axis: lax.rem(lax.axis_index(axis) + k, sizes[axis])},
                                device_id_type=pl.DeviceIdType.MESH)

    lane = lax.broadcasted_iota(i32, (rows, LANES), 1)
    number = keep[...] * fix[...]
    high, low = number // 256, lax.rem(number, 256)
    ids = routes[...]
    meta = jnp.zeros((rows, LANES), i32)
    for k in range(topk):
        meta = meta + jnp.where(lane == ids[:, k:k + 1], high[:, k:k + 1], 0)
        meta = meta + jnp.where(lane == ids[:, k:k + 1] + nd, low[:, k:k + 1], 0)
    own_pos = (me_n * nl + me_l) * span + lax.broadcasted_iota(i32, (rows, LANES), 0) * (span // rows)
    both = lens[...]
    length = jnp.where(own_pos // SEQ == 0, both[0:1, 0:1], both[0:1, 1:2])
    meta = meta + jnp.where(lane == 2 * nd, length // 256, 0) + jnp.where(lane == 2 * nd + 1, lax.rem(length, 256), 0)
    stage[...] = jnp.zeros_like(stage)
    stage[0:rows, piece:piece + LANES] = meta.astype(f32)
    for q in range(PIECES):
        stage[q * rows:(q + 1) * rows, 0:piece] = tok[:, q * piece:(q + 1) * piece].astype(f32)
    buf_a[me_l, me_n, me_d] = stage[...].astype(bf16)
    for q in range(PIECES):
        stage[q * rows:(q + 1) * rows, 0:piece] = cot[:, q * piece:(q + 1) * piece].astype(f32)
    buf_b[me_l, me_d, me_n] = stage[:, 0:piece].astype(bf16)

    pl.semaphore_wait(barrier, sum(sizes[axis] - 1 for axis in AXES))
    a.gather_first()
    b.gather_first()

    out_row = lax.broadcasted_iota(i32, (block, block), 0)
    in_row = lax.broadcasted_iota(i32, (block, block), 1)

    def place(wide, tall):
        core, node, part, j = (tall // (nn * chunk), tall // chunk % nn, tall % chunk // rows, tall % rows)
        return wide == part * group + (node * nl + core) * rows + j

    to_rows = place(out_row, in_row).astype(f32).astype(bf16)
    to_chunks = place(in_row, out_row).astype(f32).astype(bf16)
    lane_g = lax.broadcasted_iota(i32, (group, LANES), 1)
    pick_w = jnp.where(lane_g == me_d, 256.0, 0.0) + jnp.where(lane_g == me_d + nd, 1.0, 0.0)
    pick_l = jnp.where(lane_g == 2 * nd, 256.0, 0.0) + jnp.where(lane_g == 2 * nd + 1, 1.0, 0.0)
    member = lax.broadcasted_iota(i32, (group, 1), 0)
    position = member // rows * span + member % rows * (span // rows)
    second = position // SEQ
    inside = (position - second * SEQ).astype(f32)
    sign = (1 - 2 * second).astype(f32)

    def each_group(fn):
        if nd <= 4:
            for g in range(nd):
                fn(g)
        else:
            pl.loop(0, nd)(fn)

    def group_rows(g):
        return pl.ds(g * group if isinstance(g, int) else pl.multiple_of(g * group, group), group)

    def take_x(g):
        got = buf_a[:, :, g].reshape(block, piece + LANES)
        spread = jnp.dot(to_rows, got, preferred_element_type=f32)
        for q in range(PIECES):
            xs[q, group_rows(g), :] = spread[q * group:(q + 1) * group, 0:piece].astype(bf16)
        meta_g = spread[0:group, piece:]
        weight = jnp.sum(meta_g * pick_w, axis=1, keepdims=True) * (1.0 / 65536.0)
        size = jnp.sum(meta_g * pick_l, axis=1, keepdims=True)
        scale = sign * (inside < size).astype(f32) * float(SEQ) / size
        cw[group_rows(g), :] = weight
        fw[group_rows(g), :] = weight * scale

    def take_g(g):
        spread = jnp.dot(to_rows, buf_b[:, g].reshape(block, piece), preferred_element_type=f32)
        factor = fw[group_rows(g), :]
        for q in range(PIECES):
            gs[q, group_rows(g), :] = (spread[q * group:(q + 1) * group, :] * factor).astype(bf16)

    nt = (((1,), (1,)), ((), ()))
    step = min(total_rows, 128)

    def each_block(fn):
        if total_rows == step:
            fn(pl.ds(0, step))
        else:
            pl.loop(0, total_rows // step)(lambda i: fn(pl.ds(pl.multiple_of(i * step, step), step)))

    def project(rows_ref, w_ref, part):
        total = None
        for q in range(PIECES):
            term = lax.dot_general(rows_ref[q, part, :], w_ref[:, q * piece:(q + 1) * piece], nt, preferred_element_type=f32)
            total = term if total is None else total + term
        return total

    def store_back(buf_write):
        def put(g):
            rows_g = jnp.concatenate([back[q, group_rows(g), :] for q in range(PIECES)], axis=0)
            chunks = jnp.dot(to_chunks, rows_g, preferred_element_type=f32).astype(bf16)
            buf_write(g, chunks.reshape(nl, nn, chunk, piece))
        each_group(put)

    gate_s, up_s, sig_s = hid

    def forward(part):
        gate = project(xs, wg, part)
        up = project(xs, wu, part)
        sig = jax.nn.sigmoid(gate)
        gate_s[part, :], up_s[part, :], sig_s[part, :] = gate, up, sig
        hidden = (gate * sig * up).astype(bf16)
        gd[2, part, :] = hidden
        weight = cw[part, :]
        for q in range(PIECES):
            cols = slice(q * piece, (q + 1) * piece)
            back[q, part, :] = (jnp.dot(hidden, wd[:, cols], preferred_element_type=f32) * weight).astype(bf16)

    def backward(part):
        grad = project(gs, wd, part)
        gate, up, sig = gate_s[part, :], up_s[part, :], sig_s[part, :]
        gate_delta = (grad * up * (sig * (1.0 + gate * (1.0 - sig)))).astype(bf16)
        up_delta = (grad * (gate * sig)).astype(bf16)
        gd[0, part, :] = gate_delta
        for q in range(PIECES):
            cols = slice(q * piece, (q + 1) * piece)
            back[q, part, :] = (jnp.dot(gate_delta, wg[:, cols], preferred_element_type=f32)
                                + jnp.dot(up_delta, wu[:, cols], preferred_element_type=f32)).astype(bf16)

    a.gather_second()
    b.gather_second()
    a.gather_core()
    a.gathered()
    a.drain()
    for load in loads:
        load.wait()
    each_group(take_x)
    each_block(forward)

    def write_a(g, value):
        buf_a[:, :, g, :, 0:piece] = value

    def write_b(g, value):
        buf_b[:, g] = value

    store_back(write_a)
    a.sum_core(r0a)
    b.gather_core()
    b.gathered()
    b.drain()
    each_group(take_g)
    each_block(backward)
    store_back(write_b)
    b.sum_core(r0b)
    a.sum_second(r0a, r1a)
    b.sum_second(r0b, r1b)
    delta_t = gd[0].astype(f32).T.astype(bf16)
    hidden_t = gd[2].astype(f32).T.astype(bf16)
    for q in range(PIECES):
        cols = slice(q * piece, (q + 1) * piece)
        grad_gate[:, cols] = jnp.dot(delta_t, xs[q], preferred_element_type=f32).astype(bf16)
        grad_down[:, cols] = jnp.dot(hidden_t, gs[q], preferred_element_type=f32).astype(bf16)
    a.sum_first(r1a, r2a)
    b.sum_first(r1b, r2b)
    for flow, r2, out in ((a, r2a, layer_out), (b, r2b, token_grad)):
        stage[:, 0:piece] = flow.summed(r2)
        for q in range(PIECES):
            out[:, q * piece:(q + 1) * piece] = stage[q * rows:(q + 1) * rows, 0:piece].astype(bf16)
    a.drain()
    b.drain()


def body(sizes, tokens, routes, gate_fix, keep, seq_lengths, cotangent, w_gate, w_up, w_down):
    rows, width = tokens.shape
    nd, nn, nl = (sizes[a] for a in AXES)
    piece = width // PIECES
    hidden = w_gate.shape[1]
    chunk = rows * PIECES
    total = nd * nn * nl * rows
    dma = pltpu.SemaphoreType.DMA

    def flow_sems(n1, n2):
        return [dma((n1,)), dma((n1,)), dma((n2,)), dma((n2,)), dma((n2,)), dma((n2,)),
                dma((n1,)), dma((n1,)), dma((n2,)), dma((n2,)), dma, dma]

    vmem = pl.BlockSpec(memory_space=pltpu.VMEM)
    hbm = pl.BlockSpec(memory_space=pl.ANY)
    out_shape = (
        jax.ShapeDtypeStruct((rows, width), bf16),
        jax.ShapeDtypeStruct((rows, width), bf16),
        jax.ShapeDtypeStruct((hidden, width), bf16),
        jax.ShapeDtypeStruct((hidden, width), bf16),
    )
    scratch = [
        pltpu.VMEM((nl, nn, nd, chunk, piece + LANES), bf16),
        pltpu.VMEM((nl, nd, nn, chunk, piece), bf16),
        pltpu.VMEM((chunk, piece + LANES), f32),
        pltpu.VMEM((hidden, width), bf16),
        pltpu.VMEM((hidden, width), bf16),
        pltpu.VMEM((hidden, width), bf16),
        pltpu.VMEM((PIECES, total, piece), bf16),
        pltpu.VMEM((PIECES, total, piece), bf16),
        pltpu.VMEM((total, 1), f32),
        pltpu.VMEM((total, 1), f32),
        pltpu.VMEM((PIECES, total, piece), bf16),
        [pltpu.VMEM((total, hidden), f32)] * 3,
        pltpu.VMEM((3, total, hidden), bf16),
        pltpu.VMEM((nn, nd, chunk, piece), bf16),
        pltpu.VMEM((nn - 1, nd, chunk, piece), bf16),
        pltpu.VMEM((nd - 1, chunk, piece), bf16),
        pltpu.VMEM((nd, nn, chunk, piece), bf16),
        pltpu.VMEM((nd - 1, nn, chunk, piece), bf16),
        pltpu.VMEM((nn - 1, chunk, piece), bf16),
        dma((3,)),
        *flow_sems(nd, nn),
        *flow_sems(nn, nd),
    ]
    layer_out, token_grad, grad_gate, grad_down = pl.pallas_call(
        functools.partial(kernel, sizes),
        out_shape=out_shape,
        in_specs=[vmem] * 6 + [hbm] * 3,
        out_specs=(vmem,) * 4,
        scratch_shapes=scratch,
        compiler_params=pltpu.CompilerParams(
            collective_id=0, has_side_effects=True, vmem_limit_bytes=63 * 1024 * 1024
        ),
        name="experts",
    )(tokens, routes, gate_fix, keep, seq_lengths, cotangent, w_gate[0], w_up[0], w_down[0])
    return layer_out, token_grad, grad_gate[None], grad_down[None]


def solution(mesh):
    rows = P(AXES, None)
    weights = P("dp", ("node", "local"), None)
    in_specs = (rows, rows, rows, rows, P("dp", None), rows, weights, weights, weights)
    out_specs = (rows, rows, weights, weights)
    sizes = {axis: mesh.shape[axis] for axis in AXES}
    return jax.shard_map(functools.partial(body, sizes), mesh=mesh, in_specs=in_specs, out_specs=out_specs, check_vma=False)
```

```python
import functools

import jax
import jax.numpy as jnp
from jax import lax
from jax.experimental import pallas as pl
from jax.experimental.pallas import tpu as pltpu
from jax.sharding import PartitionSpec as P

SEQ = 4096
LANES = 128
PIECES = 4
AXES = ("dp", "node", "local")

bf16, f32, i32 = jnp.bfloat16, jnp.float32, jnp.int32


class Flow:
    def __init__(self, buf, first, second, sizes, width, sems):
        self.buf, self.first, self.second = buf, first, second
        self.n1, self.n2 = sizes[first], sizes[second]
        self.i1, self.i2 = lax.axis_index(first), lax.axis_index(second)
        self.core = lax.axis_index("local")
        self.width = width
        self.s1, self.q1, self.s2, self.q2, self.s0, self.q0 = sems[:6]
        self.t1, self.u1, self.t2, self.u2, self.t0, self.u0 = sems[6:]
        self.sent = []

    def push(self, src, dst, send, recv, axis, peer):
        copy = pltpu.make_async_remote_copy(
            src_ref=src, dst_ref=dst, send_sem=send, recv_sem=recv,
            device_id={axis: peer}, device_id_type=pl.DeviceIdType.MESH,
        )
        copy.start()
        self.sent.append(copy)

    def arrive(self, dst, send, recv, axis, peer):
        pltpu.make_async_remote_copy(
            src_ref=dst, dst_ref=dst, send_sem=send, recv_sem=recv,
            device_id={axis: peer}, device_id_type=pl.DeviceIdType.MESH,
        ).wait_recv()

    def drain(self):
        for copy in self.sent:
            copy.wait_send()
        self.sent = []

    def gather_first(self):
        own = self.buf.at[self.core, self.i2, self.i1]
        for k in range(1, self.n1):
            self.push(own, own, self.s1.at[k], self.q1.at[k], self.first, lax.rem(self.i1 + k, self.n1))

    def gather_second(self):
        for k in range(1, self.n1):
            source = lax.rem(self.i1 + self.n1 - k, self.n1)
            self.arrive(self.buf.at[self.core, self.i2, source], self.s1.at[k], self.q1.at[k], self.first, source)
        own = self.buf.at[self.core, self.i2]
        for k in range(1, self.n2):
            self.push(own, own, self.s2.at[k], self.q2.at[k], self.second, lax.rem(self.i2 + k, self.n2))
        self.push(own, own, self.s0.at[0], self.q0.at[0], "local", 1 - self.core)

    def gather_core(self):
        for k in range(1, self.n2):
            source = lax.rem(self.i2 + self.n2 - k, self.n2)
            block = self.buf.at[self.core, source]
            self.arrive(block, self.s2.at[k], self.q2.at[k], self.second, source)
            self.push(block, block, self.s0.at[k], self.q0.at[k], "local", 1 - self.core)

    def gathered(self):
        for k in range(self.n2):
            source = lax.rem(self.i2 + self.n2 - k, self.n2)
            block = self.buf.at[1 - self.core, source]
            self.arrive(block, self.s0.at[k], self.q0.at[k], "local", 1 - self.core)

    def lanes(self, *index):
        return self.buf.at[(*index, Ellipsis, pl.ds(0, self.width))]

    def sum_core(self, r0):
        self.push(self.lanes(1 - self.core), r0, self.t0, self.u0, "local", 1 - self.core)

    def sum_second(self, r0, r1):
        self.arrive(r0, self.t0, self.u0, "local", 1 - self.core)
        for k in list(range(1, self.n2)) + [0]:
            peer = lax.rem(self.i2 + k, self.n2)
            kept = self.lanes(self.core, peer)
            kept[...] = (kept[...].astype(f32) + r0[peer].astype(f32)).astype(bf16)
            if k:
                self.push(kept, r1.at[k - 1], self.t2.at[k], self.u2.at[k], self.second, peer)

    def sum_first(self, r1, r2):
        kept = self.lanes(self.core, self.i2)
        for k in range(1, self.n2):
            source = lax.rem(self.i2 + self.n2 - k, self.n2)
            self.arrive(r1.at[k - 1], self.t2.at[k], self.u2.at[k], self.second, source)
        total = kept[...].astype(f32)
        for k in range(1, self.n2):
            total = total + r1[k - 1].astype(f32)
        kept[...] = total.astype(bf16)
        for k in range(1, self.n1):
            peer = lax.rem(self.i1 + k, self.n1)
            self.push(self.lanes(self.core, self.i2, peer), r2.at[k - 1], self.t1.at[k], self.u1.at[k], self.first, peer)

    def summed(self, r2):
        total = self.lanes(self.core, self.i2, self.i1)[...].astype(f32)
        for k in range(1, self.n1):
            source = lax.rem(self.i1 + self.n1 - k, self.n1)
            self.arrive(r2.at[k - 1], self.t1.at[k], self.u1.at[k], self.first, source)
            total = total + r2[k - 1].astype(f32)
        return total


def kernel(sizes, tok, routes, fix, keep, lens, cot, wg_hbm, wu_hbm, wd_hbm,
           layer_hbm, token_hbm, gate_hbm, down_hbm, layer_out, token_grad, grad_gate, grad_down,
           buf_a, buf_c, buf_b, stage, wg, wu, wd, xs, gs, cw, fw, back, hid, gd,
           r0a, r1a, r2a, r0c, r1c, r2c, r0b, r1b, r2b, wsem, osem, *sems):
    nd, nn, nl = (sizes[a] for a in AXES)
    me_d, me_n, me_l = (lax.axis_index(a) for a in AXES)
    rows, width = tok.shape
    topk = routes.shape[0]
    piece = width // PIECES
    ranks = nn * nl
    group = rows * ranks
    chunk = rows * PIECES
    block = ranks * chunk
    span = 2 * SEQ // ranks
    total_rows = nd * group
    part_c, part_b = buf_c.shape[-1], buf_b.shape[-1]
    a = Flow(buf_a, "dp", "node", sizes, piece, sems[:12])
    c = Flow(buf_c, "dp", "node", sizes, part_c, sems[12:24])
    b = Flow(buf_b, "node", "dp", sizes, part_b, sems[24:])

    loads = [pltpu.make_async_copy(src, dst, wsem.at[k])
             for k, (src, dst) in enumerate(((wg_hbm, wg), (wu_hbm, wu), (wd_hbm, wd)))]
    for load in loads:
        load.start()

    barrier = pltpu.get_barrier_semaphore()
    for axis in AXES:
        for k in range(1, sizes[axis]):
            pl.semaphore_signal(barrier, inc=1, device_id={axis: lax.rem(lax.axis_index(axis) + k, sizes[axis])},
                                device_id_type=pl.DeviceIdType.MESH)

    lane = lax.broadcasted_iota(i32, (rows, LANES), 1)
    number = keep[...] * fix[...]
    diagonal = lax.broadcasted_iota(i32, (rows, rows), 0) == lax.broadcasted_iota(i32, (rows, rows), 1)

    def column(values, k):
        return jnp.sum(jnp.where(diagonal, values[k:k + 1, :], 0), axis=1, keepdims=True)

    meta = jnp.zeros((rows, LANES), i32)
    for k in range(topk):
        expert, units = column(routes[...], k), column(number, k)
        meta = meta + jnp.where(lane == expert, units // 256, 0)
        meta = meta + jnp.where(lane == expert + nd, lax.rem(units, 256), 0)
    own_pos = (me_n * nl + me_l) * span + lax.broadcasted_iota(i32, (rows, LANES), 0) * (span // rows)
    both = lens[...]
    length = jnp.where(own_pos // SEQ == 0, both[0:1, 0:1], both[0:1, 1:2])
    meta = meta + jnp.where(lane == 2 * nd, length // 256, 0) + jnp.where(lane == 2 * nd + 1, lax.rem(length, 256), 0)
    stage[...] = jnp.zeros_like(stage)
    stage[0:rows, piece:piece + LANES] = meta.astype(f32)
    for q in range(PIECES):
        stage[q * rows:(q + 1) * rows, 0:piece] = tok[:, q * piece:(q + 1) * piece].astype(f32)
    buf_a[me_l, me_n, me_d] = stage[...].astype(bf16)
    for q in range(PIECES):
        stage[q * rows:(q + 1) * rows, 0:piece] = cot[:, q * piece:(q + 1) * piece].astype(f32)
    buf_c[me_l, me_n, me_d] = stage[:, 0:part_c].astype(bf16)
    buf_b[me_l, me_d, me_n] = stage[:, part_c:piece].astype(bf16)

    pl.semaphore_wait(barrier, sum(sizes[axis] - 1 for axis in AXES))
    a.gather_first()
    b.gather_first()
    c.gather_first()

    out_row = lax.broadcasted_iota(i32, (block, block), 0)
    in_row = lax.broadcasted_iota(i32, (block, block), 1)

    def place(wide, tall):
        core, node, part, j = (tall // (nn * chunk), tall // chunk % nn, tall % chunk // rows, tall % rows)
        return wide == part * group + (node * nl + core) * rows + j

    to_rows = place(out_row, in_row).astype(f32).astype(bf16)
    to_chunks = place(in_row, out_row).astype(f32).astype(bf16)
    lane_g = lax.broadcasted_iota(i32, (group, LANES), 1)
    pick_w = jnp.where(lane_g == me_d, 256.0, 0.0) + jnp.where(lane_g == me_d + nd, 1.0, 0.0)
    pick_l = jnp.where(lane_g == 2 * nd, 256.0, 0.0) + jnp.where(lane_g == 2 * nd + 1, 1.0, 0.0)
    member = lax.broadcasted_iota(i32, (group, 1), 0)
    position = member // rows * span + member % rows * (span // rows)
    second = position // SEQ
    inside = (position - second * SEQ).astype(f32)
    sign = (1 - 2 * second).astype(f32)

    def each_group(fn):
        if nd <= 4:
            for g in range(nd):
                fn(g)
        else:
            pl.loop(0, nd)(fn)

    def group_rows(g):
        return pl.ds(g * group if isinstance(g, int) else pl.multiple_of(g * group, group), group)

    def take_x(g):
        got = buf_a[:, :, g].reshape(block, piece + LANES)
        spread = jnp.dot(to_rows, got, preferred_element_type=f32)
        for q in range(PIECES):
            xs[q, group_rows(g), :] = spread[q * group:(q + 1) * group, 0:piece].astype(bf16)
        meta_g = spread[0:group, piece:]
        weight = jnp.sum(meta_g * pick_w, axis=1, keepdims=True) * (1.0 / 65536.0)
        size = jnp.sum(meta_g * pick_l, axis=1, keepdims=True)
        scale = sign * (inside < size).astype(f32) * float(SEQ) / size
        cw[group_rows(g), :] = weight
        fw[group_rows(g), :] = weight * scale

    def take_g(g):
        factor = fw[group_rows(g), :]
        for got, start, size in ((buf_c[:, :, g], 0, part_c), (buf_b[:, g], part_c, part_b)):
            spread = jnp.dot(to_rows, got.reshape(block, size), preferred_element_type=f32)
            for q in range(PIECES):
                gs[q, group_rows(g), start:start + size] = (spread[q * group:(q + 1) * group, :] * factor).astype(bf16)

    nt = (((1,), (1,)), ((), ()))
    step = min(total_rows, 128)

    def each_block(fn):
        if total_rows == step:
            fn(pl.ds(0, step))
        else:
            pl.loop(0, total_rows // step)(lambda i: fn(pl.ds(pl.multiple_of(i * step, step), step)))

    def project(rows_ref, w_ref, part):
        total = None
        for q in range(PIECES):
            term = lax.dot_general(rows_ref[q, part, :], w_ref[:, q * piece:(q + 1) * piece], nt, preferred_element_type=f32)
            total = term if total is None else total + term
        return total

    def store_back(buf_write):
        def put(g):
            rows_g = jnp.concatenate([back[q, group_rows(g), :] for q in range(PIECES)], axis=0)
            chunks = jnp.dot(to_chunks, rows_g, preferred_element_type=f32).astype(bf16)
            buf_write(g, chunks.reshape(nl, nn, chunk, piece))
        each_group(put)

    gate_s, up_s, sig_s = hid

    def forward(part):
        gate = project(xs, wg, part)
        up = project(xs, wu, part)
        sig = jax.nn.sigmoid(gate)
        gate_s[part, :], up_s[part, :], sig_s[part, :] = gate, up, sig
        gd[2, part, :] = (gate * sig * up).astype(bf16)

    def outward(part):
        hidden = gd[2, part, :]
        weight = cw[part, :]
        for q in range(PIECES):
            cols = slice(q * piece, (q + 1) * piece)
            back[q, part, :] = (jnp.dot(hidden, wd[:, cols], preferred_element_type=f32) * weight).astype(bf16)

    def backward(part):
        grad = project(gs, wd, part)
        gate, up, sig = gate_s[part, :], up_s[part, :], sig_s[part, :]
        gate_delta = (grad * up * (sig * (1.0 + gate * (1.0 - sig)))).astype(bf16)
        up_delta = (grad * (gate * sig)).astype(bf16)
        gd[0, part, :] = gate_delta
        for q in range(PIECES):
            cols = slice(q * piece, (q + 1) * piece)
            back[q, part, :] = (jnp.dot(gate_delta, wg[:, cols], preferred_element_type=f32)
                                + jnp.dot(up_delta, wu[:, cols], preferred_element_type=f32)).astype(bf16)

    a.gather_second()
    b.gather_second()
    c.gather_second()
    for load in loads:
        load.wait()
    a.gather_core()
    a.gathered()
    each_group(take_x)
    each_block(forward)
    c.gather_core()
    b.gather_core()
    each_block(outward)

    def write_a(g, value):
        buf_a[:, :, g, :, 0:piece] = value

    def write_b(g, value):
        buf_c[:, :, g] = value[..., 0:part_c]
        buf_b[:, g] = value[..., part_c:]

    a.drain()
    store_back(write_a)
    a.sum_core(r0a)
    c.gathered()
    b.gathered()
    each_group(take_g)
    a.sum_second(r0a, r1a)
    each_block(backward)
    c.drain()
    b.drain()
    store_back(write_b)
    b.sum_core(r0b)
    c.sum_core(r0c)
    b.sum_second(r0b, r1b)
    c.sum_second(r0c, r1c)
    delta_t = gd[0].astype(f32).T.astype(bf16)
    hidden_t = gd[2].astype(f32).T.astype(bf16)
    for q in range(PIECES):
        cols = slice(q * piece, (q + 1) * piece)
        grad_gate[:, cols] = jnp.dot(delta_t, xs[q], preferred_element_type=f32).astype(bf16)
        grad_down[:, cols] = jnp.dot(hidden_t, gs[q], preferred_element_type=f32).astype(bf16)
    stores = [pltpu.make_async_copy(src, dst, osem.at[k])
              for k, (src, dst) in enumerate(((grad_gate, gate_hbm), (grad_down, down_hbm),
                                              (layer_out, layer_hbm), (token_grad, token_hbm)))]
    stores[0].start()
    stores[1].start()
    a.sum_first(r1a, r2a)
    b.sum_first(r1b, r2b)
    c.sum_first(r1c, r2c)

    def finish(out, store):
        for q in range(PIECES):
            out[:, q * piece:(q + 1) * piece] = stage[q * rows:(q + 1) * rows, 0:piece].astype(bf16)
        store.start()

    stage[:, 0:piece] = a.summed(r2a)
    finish(layer_out, stores[2])
    stage[:, part_c:piece] = b.summed(r2b)
    stage[:, 0:part_c] = c.summed(r2c)
    finish(token_grad, stores[3])
    for flow in (a, b, c):
        flow.drain()
    for store in stores:
        store.wait()


def hand_on(*refs):
    count = len(refs) // 2
    for src, dst in zip(refs[:count], refs[count:]):
        dst[...] = src[...]


def body(sizes, tokens, routes, gate_fix, keep, seq_lengths, cotangent, w_gate, w_up, w_down):
    rows, width = tokens.shape
    nd, nn, nl = (sizes[a] for a in AXES)
    piece = width // PIECES
    hidden = w_gate.shape[1]
    chunk = rows * PIECES
    part_c = piece // LANES * 4 // 7 * LANES
    part_b = piece - part_c
    total = nd * nn * nl * rows
    dma = pltpu.SemaphoreType.DMA

    def flow_sems(n1, n2):
        return [dma((n1,)), dma((n1,)), dma((n2,)), dma((n2,)), dma((n2,)), dma((n2,)),
                dma((n1,)), dma((n1,)), dma((n2,)), dma((n2,)), dma, dma]

    vmem = pl.BlockSpec(memory_space=pltpu.VMEM)
    hbm = pl.BlockSpec(memory_space=pl.ANY)
    out_shape = (
        jax.ShapeDtypeStruct((rows, width), bf16),
        jax.ShapeDtypeStruct((rows, width), bf16),
        jax.ShapeDtypeStruct((hidden, width), bf16),
        jax.ShapeDtypeStruct((hidden, width), bf16),
    )
    scratch = [
        pltpu.VMEM((rows, width), bf16),
        pltpu.VMEM((rows, width), bf16),
        pltpu.VMEM((hidden, width), bf16),
        pltpu.VMEM((hidden, width), bf16),
        pltpu.VMEM((nl, nn, nd, chunk, piece + LANES), bf16),
        pltpu.VMEM((nl, nn, nd, chunk, part_c), bf16),
        pltpu.VMEM((nl, nd, nn, chunk, part_b), bf16),
        pltpu.VMEM((chunk, piece + LANES), f32),
        pltpu.VMEM((hidden, width), bf16),
        pltpu.VMEM((hidden, width), bf16),
        pltpu.VMEM((hidden, width), bf16),
        pltpu.VMEM((PIECES, total, piece), bf16),
        pltpu.VMEM((PIECES, total, piece), bf16),
        pltpu.VMEM((total, 1), f32),
        pltpu.VMEM((total, 1), f32),
        pltpu.VMEM((PIECES, total, piece), bf16),
        [pltpu.VMEM((total, hidden), f32)] * 3,
        pltpu.VMEM((3, total, hidden), bf16),
        pltpu.VMEM((nn, nd, chunk, piece), bf16),
        pltpu.VMEM((nn - 1, nd, chunk, piece), bf16),
        pltpu.VMEM((nd - 1, chunk, piece), bf16),
        pltpu.VMEM((nn, nd, chunk, part_c), bf16),
        pltpu.VMEM((nn - 1, nd, chunk, part_c), bf16),
        pltpu.VMEM((nd - 1, chunk, part_c), bf16),
        pltpu.VMEM((nd, nn, chunk, part_b), bf16),
        pltpu.VMEM((nd - 1, nn, chunk, part_b), bf16),
        pltpu.VMEM((nn - 1, chunk, part_b), bf16),
        dma((3,)),
        dma((4,)),
        *flow_sems(nd, nn),
        *flow_sems(nd, nn),
        *flow_sems(nn, nd),
    ]
    results = pl.pallas_call(
        functools.partial(kernel, sizes),
        out_shape=out_shape,
        in_specs=[vmem] * 6 + [hbm] * 3,
        out_specs=(hbm,) * 4,
        scratch_shapes=scratch,
        compiler_params=pltpu.CompilerParams(
            collective_id=0, has_side_effects=True, vmem_limit_bytes=63 * 1024 * 1024
        ),
        name="experts",
    )(tokens, routes.T, gate_fix.T, keep.T, seq_lengths, cotangent, w_gate[0], w_up[0], w_down[0])
    layer_out, token_grad, grad_gate, grad_down = pl.pallas_call(
        hand_on, out_shape=out_shape, in_specs=[vmem] * 4, out_specs=(vmem,) * 4, name="hand_on",
    )(*results)
    return layer_out, token_grad, grad_gate[None], grad_down[None]


def solution(mesh):
    rows = P(AXES, None)
    weights = P("dp", ("node", "local"), None)
    in_specs = (rows, rows, rows, rows, P("dp", None), rows, weights, weights, weights)
    out_specs = (rows, rows, weights, weights)
    sizes = {axis: mesh.shape[axis] for axis in AXES}
    return jax.shard_map(functools.partial(body, sizes), mesh=mesh, in_specs=in_specs, out_specs=out_specs, check_vma=False)
```

```python
import functools

import jax
import jax.numpy as jnp
from jax import lax
from jax.experimental import pallas as pl
from jax.experimental.pallas import tpu as pltpu
from jax.sharding import PartitionSpec as P

SEQ = 4096
LANES = 128
PIECES = 4
AXES = ("dp", "node", "local")

bf16, f32, i32 = jnp.bfloat16, jnp.float32, jnp.int32


class Flow:
    def __init__(self, buf, first, second, sizes, width, sems):
        self.buf, self.first, self.second = buf, first, second
        self.n1, self.n2 = sizes[first], sizes[second]
        self.i1, self.i2 = lax.axis_index(first), lax.axis_index(second)
        self.core = lax.axis_index("local")
        self.width = width
        self.s1, self.q1, self.s2, self.q2, self.s0, self.q0 = sems[:6]
        self.t1, self.u1, self.t2, self.u2, self.t0, self.u0 = sems[6:]
        self.sent = []

    def push(self, src, dst, send, recv, axis, peer):
        copy = pltpu.make_async_remote_copy(
            src_ref=src, dst_ref=dst, send_sem=send, recv_sem=recv,
            device_id={axis: peer}, device_id_type=pl.DeviceIdType.MESH,
        )
        copy.start()
        self.sent.append(copy)

    def arrive(self, dst, send, recv, axis, peer):
        pltpu.make_async_remote_copy(
            src_ref=dst, dst_ref=dst, send_sem=send, recv_sem=recv,
            device_id={axis: peer}, device_id_type=pl.DeviceIdType.MESH,
        ).wait_recv()

    def drain(self):
        for copy in self.sent:
            copy.wait_send()
        self.sent = []

    def gather_first(self):
        own = self.buf.at[self.core, self.i2, self.i1]
        for k in range(1, self.n1):
            self.push(own, own, self.s1.at[k], self.q1.at[k], self.first, lax.rem(self.i1 + k, self.n1))
        self.pass_on(0)

    def pass_on(self, step):
        chunk = self.buf.at[self.core, self.i2, lax.rem(self.i1 + self.n1 - step, self.n1)]
        for k in range(1, self.n2):
            self.push(chunk, chunk, self.s2.at[k, step], self.q2.at[k], self.second, lax.rem(self.i2 + k, self.n2))

    def gather_second(self):
        for k in range(1, self.n1):
            source = lax.rem(self.i1 + self.n1 - k, self.n1)
            self.arrive(self.buf.at[self.core, self.i2, source], self.s1.at[k], self.q1.at[k], self.first, source)
            self.pass_on(k)
        own = self.buf.at[self.core, self.i2]
        self.push(own, own, self.s0.at[0], self.q0.at[0], "local", 1 - self.core)

    def gather_core(self):
        for k in range(1, self.n2):
            source = lax.rem(self.i2 + self.n2 - k, self.n2)
            block = self.buf.at[self.core, source]
            self.arrive(block, self.s2.at[k, 0], self.q2.at[k], self.second, source)
            self.push(block, block, self.s0.at[k], self.q0.at[k], "local", 1 - self.core)

    def gathered(self):
        for k in range(self.n2):
            source = lax.rem(self.i2 + self.n2 - k, self.n2)
            block = self.buf.at[1 - self.core, source]
            self.arrive(block, self.s0.at[k], self.q0.at[k], "local", 1 - self.core)

    def lanes(self, *index):
        return self.buf.at[(*index, Ellipsis, pl.ds(0, self.width))]

    def sum_core(self, r0):
        for k in list(range(1, self.n2)) + [0]:
            peer = lax.rem(self.i2 + k, self.n2)
            self.push(self.lanes(1 - self.core, peer), r0.at[peer], self.t0.at[k], self.u0.at[k], "local", 1 - self.core)

    def sum_second(self, r0, r1):
        for k in list(range(1, self.n2)) + [0]:
            peer = lax.rem(self.i2 + k, self.n2)
            self.arrive(r0.at[peer], self.t0.at[k], self.u0.at[k], "local", 1 - self.core)
            kept = self.lanes(self.core, peer)
            kept[...] = (kept[...].astype(f32) + r0[peer].astype(f32)).astype(bf16)
            if k:
                for j in list(range(1, self.n1)) + [0]:
                    goal = lax.rem(self.i1 + j, self.n1)
                    self.push(self.lanes(self.core, peer, goal), r1.at[k - 1, goal],
                              self.t2.at[k, j], self.u2.at[k, j], self.second, peer)

    def sum_first(self, r1, r2):
        for j in list(range(1, self.n1)) + [0]:
            goal = lax.rem(self.i1 + j, self.n1)
            kept = self.lanes(self.core, self.i2, goal)
            total = kept[...].astype(f32)
            for k in range(1, self.n2):
                source = lax.rem(self.i2 + self.n2 - k, self.n2)
                self.arrive(r1.at[k - 1, goal], self.t2.at[k, j], self.u2.at[k, j], self.second, source)
                total = total + r1[k - 1, goal].astype(f32)
            kept[...] = total.astype(bf16)
            if j:
                self.push(kept, r2.at[j - 1], self.t1.at[j], self.u1.at[j], self.first, goal)

    def summed(self, r2):
        total = self.lanes(self.core, self.i2, self.i1)[...].astype(f32)
        for k in range(1, self.n1):
            source = lax.rem(self.i1 + self.n1 - k, self.n1)
            self.arrive(r2.at[k - 1], self.t1.at[k], self.u1.at[k], self.first, source)
            total = total + r2[k - 1].astype(f32)
        return total


def kernel(sizes, tok, routes, fix, keep, lens, cot, wg_hbm, wu_hbm, wd_hbm,
           layer_hbm, token_hbm, gate_hbm, down_hbm, layer_out, token_grad, grad_gate, grad_down,
           buf_a, buf_c, buf_b, stage, wg, wu, wd, xs, gs, cw, fw, back, hid, gd,
           r0a, r1a, r2a, r0c, r1c, r2c, r0b, r1b, r2b, wsem, osem, *sems):
    nd, nn, nl = (sizes[a] for a in AXES)
    me_d, me_n, me_l = (lax.axis_index(a) for a in AXES)
    rows, width = tok.shape
    topk = routes.shape[0]
    piece = width // PIECES
    ranks = nn * nl
    group = rows * ranks
    chunk = rows * PIECES
    block = ranks * chunk
    span = 2 * SEQ // ranks
    total_rows = nd * group
    part_c, part_b = buf_c.shape[-1], buf_b.shape[-1]
    a = Flow(buf_a, "dp", "node", sizes, piece, sems[:12])
    c = Flow(buf_c, "dp", "node", sizes, part_c, sems[12:24])
    b = Flow(buf_b, "node", "dp", sizes, part_b, sems[24:])

    loads = [pltpu.make_async_copy(src, dst, wsem.at[k])
             for k, (src, dst) in enumerate(((wg_hbm, wg), (wu_hbm, wu), (wd_hbm, wd)))]
    for load in loads:
        load.start()

    barrier = pltpu.get_barrier_semaphore()
    for axis in AXES:
        for k in range(1, sizes[axis]):
            pl.semaphore_signal(barrier, inc=1, device_id={axis: lax.rem(lax.axis_index(axis) + k, sizes[axis])},
                                device_id_type=pl.DeviceIdType.MESH)

    lane = lax.broadcasted_iota(i32, (rows, LANES), 1)
    number = keep[...] * fix[...]
    diagonal = lax.broadcasted_iota(i32, (rows, rows), 0) == lax.broadcasted_iota(i32, (rows, rows), 1)

    def column(values, k):
        return jnp.sum(jnp.where(diagonal, values[k:k + 1, :], 0), axis=1, keepdims=True)

    meta = jnp.zeros((rows, LANES), i32)
    for k in range(topk):
        expert, units = column(routes[...], k), column(number, k)
        meta = meta + jnp.where(lane == expert, units // 256, 0)
        meta = meta + jnp.where(lane == expert + nd, lax.rem(units, 256), 0)
    own_pos = (me_n * nl + me_l) * span + lax.broadcasted_iota(i32, (rows, LANES), 0) * (span // rows)
    both = lens[...]
    length = jnp.where(own_pos // SEQ == 0, both[0:1, 0:1], both[0:1, 1:2])
    meta = meta + jnp.where(lane == 2 * nd, length // 256, 0) + jnp.where(lane == 2 * nd + 1, lax.rem(length, 256), 0)
    stage[...] = jnp.zeros_like(stage)
    stage[0:rows, piece:piece + LANES] = meta.astype(f32)
    for q in range(PIECES):
        stage[q * rows:(q + 1) * rows, 0:piece] = tok[:, q * piece:(q + 1) * piece].astype(f32)
    buf_a[me_l, me_n, me_d] = stage[...].astype(bf16)
    for q in range(PIECES):
        stage[q * rows:(q + 1) * rows, 0:piece] = cot[:, q * piece:(q + 1) * piece].astype(f32)
    buf_c[me_l, me_n, me_d] = stage[:, 0:part_c].astype(bf16)
    buf_b[me_l, me_d, me_n] = stage[:, part_c:piece].astype(bf16)

    pl.semaphore_wait(barrier, sum(sizes[axis] - 1 for axis in AXES))
    a.gather_first()
    b.gather_first()
    c.gather_first()

    out_row = lax.broadcasted_iota(i32, (block, block), 0)
    in_row = lax.broadcasted_iota(i32, (block, block), 1)

    def place(wide, tall):
        core, node, part, j = (tall // (nn * chunk), tall // chunk % nn, tall % chunk // rows, tall % rows)
        return wide == part * group + (node * nl + core) * rows + j

    to_rows = place(out_row, in_row).astype(f32).astype(bf16)
    to_chunks = place(in_row, out_row).astype(f32).astype(bf16)
    lane_g = lax.broadcasted_iota(i32, (group, LANES), 1)
    pick_w = jnp.where(lane_g == me_d, 256.0, 0.0) + jnp.where(lane_g == me_d + nd, 1.0, 0.0)
    pick_l = jnp.where(lane_g == 2 * nd, 256.0, 0.0) + jnp.where(lane_g == 2 * nd + 1, 1.0, 0.0)
    member = lax.broadcasted_iota(i32, (group, 1), 0)
    position = member // rows * span + member % rows * (span // rows)
    second = position // SEQ
    inside = (position - second * SEQ).astype(f32)
    sign = (1 - 2 * second).astype(f32)

    def each_group(fn):
        if nd <= 4:
            for g in range(nd):
                fn(g)
        else:
            pl.loop(0, nd)(fn)

    def group_rows(g):
        return pl.ds(g * group if isinstance(g, int) else pl.multiple_of(g * group, group), group)

    def take_x(g):
        got = buf_a[:, :, g].reshape(block, piece + LANES)
        spread = jnp.dot(to_rows, got, preferred_element_type=f32)
        for q in range(PIECES):
            xs[q, group_rows(g), :] = spread[q * group:(q + 1) * group, 0:piece].astype(bf16)
        meta_g = spread[0:group, piece:]
        weight = jnp.sum(meta_g * pick_w, axis=1, keepdims=True) * (1.0 / 65536.0)
        size = jnp.sum(meta_g * pick_l, axis=1, keepdims=True)
        scale = sign * (inside < size).astype(f32) * float(SEQ) / size
        cw[group_rows(g), :] = weight
        fw[group_rows(g), :] = weight * scale

    def take_g(g):
        factor = fw[group_rows(g), :]
        for got, start, size in ((buf_c[:, :, g], 0, part_c), (buf_b[:, g], part_c, part_b)):
            spread = jnp.dot(to_rows, got.reshape(block, size), preferred_element_type=f32)
            for q in range(PIECES):
                gs[q, group_rows(g), start:start + size] = (spread[q * group:(q + 1) * group, :] * factor).astype(bf16)

    nt = (((1,), (1,)), ((), ()))
    step = min(total_rows, 128)

    def each_block(fn):
        if total_rows == step:
            fn(pl.ds(0, step))
        else:
            pl.loop(0, total_rows // step)(lambda i: fn(pl.ds(pl.multiple_of(i * step, step), step)))

    def project(rows_ref, w_ref, part):
        total = None
        for q in range(PIECES):
            term = lax.dot_general(rows_ref[q, part, :], w_ref[:, q * piece:(q + 1) * piece], nt, preferred_element_type=f32)
            total = term if total is None else total + term
        return total

    def store_back(buf_write):
        def put(g):
            rows_g = jnp.concatenate([back[q, group_rows(g), :] for q in range(PIECES)], axis=0)
            chunks = jnp.dot(to_chunks, rows_g, preferred_element_type=f32).astype(bf16)
            buf_write(g, chunks.reshape(nl, nn, chunk, piece))
        each_group(put)

    gate_s, up_s, sig_s = hid

    def forward(part):
        gate = project(xs, wg, part)
        up = project(xs, wu, part)
        sig = jax.nn.sigmoid(gate)
        gate_s[part, :], up_s[part, :], sig_s[part, :] = gate, up, sig
        gd[2, part, :] = (gate * sig * up).astype(bf16)

    def outward(part):
        hidden = gd[2, part, :]
        weight = cw[part, :]
        for q in range(PIECES):
            cols = slice(q * piece, (q + 1) * piece)
            back[q, part, :] = (jnp.dot(hidden, wd[:, cols], preferred_element_type=f32) * weight).astype(bf16)

    def backward(part):
        grad = project(gs, wd, part)
        gate, up, sig = gate_s[part, :], up_s[part, :], sig_s[part, :]
        gate_delta = (grad * up * (sig * (1.0 + gate * (1.0 - sig)))).astype(bf16)
        up_delta = (grad * (gate * sig)).astype(bf16)
        gd[0, part, :] = gate_delta
        for q in range(PIECES):
            cols = slice(q * piece, (q + 1) * piece)
            back[q, part, :] = (jnp.dot(gate_delta, wg[:, cols], preferred_element_type=f32)
                                + jnp.dot(up_delta, wu[:, cols], preferred_element_type=f32)).astype(bf16)

    a.gather_second()
    b.gather_second()
    c.gather_second()
    for load in loads:
        load.wait()
    a.gather_core()
    a.gathered()
    each_group(take_x)
    each_block(forward)
    c.gather_core()
    b.gather_core()
    each_block(outward)

    def write_a(g, value):
        buf_a[:, :, g, :, 0:piece] = value

    def write_b(g, value):
        buf_c[:, :, g] = value[..., 0:part_c]
        buf_b[:, g] = value[..., part_c:]

    a.drain()
    store_back(write_a)
    a.sum_core(r0a)
    c.gathered()
    b.gathered()
    each_group(take_g)
    a.sum_second(r0a, r1a)
    each_block(backward)
    c.drain()
    b.drain()
    store_back(write_b)
    b.sum_core(r0b)
    c.sum_core(r0c)
    b.sum_second(r0b, r1b)
    c.sum_second(r0c, r1c)
    delta_t = gd[0].astype(f32).T.astype(bf16)
    hidden_t = gd[2].astype(f32).T.astype(bf16)
    for q in range(PIECES):
        cols = slice(q * piece, (q + 1) * piece)
        grad_gate[:, cols] = jnp.dot(delta_t, xs[q], preferred_element_type=f32).astype(bf16)
        grad_down[:, cols] = jnp.dot(hidden_t, gs[q], preferred_element_type=f32).astype(bf16)
    stores = [pltpu.make_async_copy(src, dst, osem.at[k])
              for k, (src, dst) in enumerate(((grad_gate, gate_hbm), (grad_down, down_hbm),
                                              (layer_out, layer_hbm), (token_grad, token_hbm)))]
    stores[0].start()
    stores[1].start()
    a.sum_first(r1a, r2a)
    b.sum_first(r1b, r2b)
    c.sum_first(r1c, r2c)

    def finish(out, store):
        for q in range(PIECES):
            out[:, q * piece:(q + 1) * piece] = stage[q * rows:(q + 1) * rows, 0:piece].astype(bf16)
        store.start()

    stage[:, 0:piece] = a.summed(r2a)
    finish(layer_out, stores[2])
    stage[:, part_c:piece] = b.summed(r2b)
    stage[:, 0:part_c] = c.summed(r2c)
    finish(token_grad, stores[3])
    for flow in (a, b, c):
        flow.drain()
    for store in stores:
        store.wait()


def hand_on(*refs):
    count = len(refs) // 2
    for src, dst in zip(refs[:count], refs[count:]):
        dst[...] = src[...]


def body(sizes, tokens, routes, gate_fix, keep, seq_lengths, cotangent, w_gate, w_up, w_down):
    rows, width = tokens.shape
    nd, nn, nl = (sizes[a] for a in AXES)
    piece = width // PIECES
    hidden = w_gate.shape[1]
    chunk = rows * PIECES
    part_c = piece // LANES * 4 // 7 * LANES
    part_b = piece - part_c
    total = nd * nn * nl * rows
    dma = pltpu.SemaphoreType.DMA

    def flow_sems(n1, n2):
        return [dma((n1,)), dma((n1,)), dma((n2, n1)), dma((n2,)), dma((n2,)), dma((n2,)),
                dma((n1,)), dma((n1,)), dma((n2, n1)), dma((n2, n1)), dma((n2,)), dma((n2,))]

    vmem = pl.BlockSpec(memory_space=pltpu.VMEM)
    hbm = pl.BlockSpec(memory_space=pl.ANY)
    out_shape = (
        jax.ShapeDtypeStruct((rows, width), bf16),
        jax.ShapeDtypeStruct((rows, width), bf16),
        jax.ShapeDtypeStruct((hidden, width), bf16),
        jax.ShapeDtypeStruct((hidden, width), bf16),
    )
    scratch = [
        pltpu.VMEM((rows, width), bf16),
        pltpu.VMEM((rows, width), bf16),
        pltpu.VMEM((hidden, width), bf16),
        pltpu.VMEM((hidden, width), bf16),
        pltpu.VMEM((nl, nn, nd, chunk, piece + LANES), bf16),
        pltpu.VMEM((nl, nn, nd, chunk, part_c), bf16),
        pltpu.VMEM((nl, nd, nn, chunk, part_b), bf16),
        pltpu.VMEM((chunk, piece + LANES), f32),
        pltpu.VMEM((hidden, width), bf16),
        pltpu.VMEM((hidden, width), bf16),
        pltpu.VMEM((hidden, width), bf16),
        pltpu.VMEM((PIECES, total, piece), bf16),
        pltpu.VMEM((PIECES, total, piece), bf16),
        pltpu.VMEM((total, 1), f32),
        pltpu.VMEM((total, 1), f32),
        pltpu.VMEM((PIECES, total, piece), bf16),
        [pltpu.VMEM((total, hidden), f32)] * 3,
        pltpu.VMEM((3, total, hidden), bf16),
        pltpu.VMEM((nn, nd, chunk, piece), bf16),
        pltpu.VMEM((nn - 1, nd, chunk, piece), bf16),
        pltpu.VMEM((nd - 1, chunk, piece), bf16),
        pltpu.VMEM((nn, nd, chunk, part_c), bf16),
        pltpu.VMEM((nn - 1, nd, chunk, part_c), bf16),
        pltpu.VMEM((nd - 1, chunk, part_c), bf16),
        pltpu.VMEM((nd, nn, chunk, part_b), bf16),
        pltpu.VMEM((nd - 1, nn, chunk, part_b), bf16),
        pltpu.VMEM((nn - 1, chunk, part_b), bf16),
        dma((3,)),
        dma((4,)),
        *flow_sems(nd, nn),
        *flow_sems(nd, nn),
        *flow_sems(nn, nd),
    ]
    results = pl.pallas_call(
        functools.partial(kernel, sizes),
        out_shape=out_shape,
        in_specs=[vmem] * 6 + [hbm] * 3,
        out_specs=(hbm,) * 4,
        scratch_shapes=scratch,
        compiler_params=pltpu.CompilerParams(
            collective_id=0, has_side_effects=True, vmem_limit_bytes=63 * 1024 * 1024
        ),
        name="experts",
    )(tokens, routes.T, gate_fix.T, keep.T, seq_lengths, cotangent, w_gate[0], w_up[0], w_down[0])
    layer_out, token_grad, grad_gate, grad_down = pl.pallas_call(
        hand_on, out_shape=out_shape, in_specs=[vmem] * 4, out_specs=(vmem,) * 4, name="hand_on",
    )(*results)
    return layer_out, token_grad, grad_gate[None], grad_down[None]


def solution(mesh):
    rows = P(AXES, None)
    weights = P("dp", ("node", "local"), None)
    in_specs = (rows, rows, rows, rows, P("dp", None), rows, weights, weights, weights)
    out_specs = (rows, rows, weights, weights)
    sizes = {axis: mesh.shape[axis] for axis in AXES}
    return jax.shard_map(functools.partial(body, sizes), mesh=mesh, in_specs=in_specs, out_specs=out_specs, check_vma=False)
```
